256 devices in a mesh: group: 16 (over x, y_hi, core), fsdp: 16 (over z, y_lo).
Axes of the slice: x: 4, y: 4 (y_hi: 2, y_lo: 2; y = y_hi * 2 + y_lo), z: 8, core: 2. Of those that a mesh axis runs over, the one named last changes fastest.
Arguments:
- features: bfloat16 [16, 4096, 5120], P('group', 'fsdp'), may hold values from -6 to 6
- value_cotangent: bfloat16 [16, 4096, 1024], P('group', 'fsdp'), may hold values from -6 to 6
- params: float32 [16, 5120, 1024], P('group', 'fsdp'), may hold values from -0.078125 to 0.078125
- momentum: float32 [16, 5120, 1024], P('group', 'fsdp'), may hold values from -0.12 to 0.12
- step_index: int32 [1], replicated, may hold values from 0 to 999
Outputs:
- input_grad: bfloat16 [16, 4096, 5120], P('group', 'fsdp')
- new_params: float32 [16, 5120, 1024], P('group', 'fsdp')
- new_momentum: float32 [16, 5120, 1024], P('group', 'fsdp')
The draws below stay inside these ranges and needn't reach their ends.
All inputs are finite; a program needn't handle non-finite values.
Results may differ from the reference program's by a relative error of at most 0.0049.
Values may be sent and summed in bfloat16 or wider, within the bound.
No kernel may reach another device: no remote copies, remote signals or barrier semaphores. Data moves between devices by JAX's collectives and lax.ppermute only.
A program may use at most 128 MiB of HBM per device.

```python
import jax
import jax.numpy as jnp
from jax import lax

D = 5120
KVW = 1024
TOKENS = 4096
N_GROUP = 16


def level_of(stream_key, shape, shards, least, largest):
    def one(dim, shards_of):
        draws = jax.random.uniform(jax.random.fold_in(jax.random.fold_in(stream_key, 6), dim), (shards_of,), jnp.float32, least / len(shards), largest / len(shards))
        return jnp.repeat(jnp.exp(draws), shape[dim] // shards_of).reshape((-1,) + (1,) * (len(shape) - dim - 1))

    level = one(*shards[0])
    for cut in shards[1:]:
        level = level * one(*cut)
    return level


def gaussian(own_key, extent, width, reach, split=(), kind=jnp.bfloat16):
    entries = width * jax.random.normal(own_key, extent, jnp.float32)
    if split:
        entries = entries * level_of(own_key, extent, split, -0.22, 0.18)
    return jnp.clip(entries, -reach, reach).astype(kind)


def setup_inputs(seed: int = 0) -> dict:
    arg_keys = jax.random.split(jax.random.key(seed), 6)
    features = gaussian(arg_keys[0], (N_GROUP, TOKENS, D), 1.0, 6.0, ((0, 16), (1, 16)))
    value_cotangent = gaussian(arg_keys[1], (N_GROUP, TOKENS, KVW), 1.0, 6.0, ((0, 16), (1, 16)))
    params = gaussian(arg_keys[2], (N_GROUP, D, KVW), D ** -0.5, 0.078125, ((0, 16), (1, 16)), jnp.float32)
    momentum = gaussian(arg_keys[3], (N_GROUP, D, KVW), 0.02, 0.12, ((0, 16), (1, 16)), jnp.float32)
    step_index = jax.random.randint(arg_keys[4], (1,), 0, 1000).astype(jnp.int32)
    return {"features": features, "value_cotangent": value_cotangent, "params": params, "momentum": momentum, "step_index": step_index}


def one_replica(pieces):
    feats, cotan, weights, moment = pieces
    weight_bf = weights.astype(jnp.bfloat16)
    input_grad = jnp.dot(cotan, weight_bf.T, preferred_element_type=jnp.float32).astype(jnp.bfloat16)
    gradient = jnp.dot(feats.T, cotan, preferred_element_type=jnp.float32) / TOKENS
    new_momentum = 0.9 * moment + gradient
    stepped = weights - 0.5 * new_momentum
    return input_grad, new_momentum, stepped


def reference(features, value_cotangent, params, momentum, step_index):
    input_grad, new_momentum, stepped = lax.map(one_replica, (features, value_cotangent, params, momentum))
    levels = N_GROUP.bit_length() - 1
    hop = jnp.left_shift(jnp.int32(1), (step_index[0] % levels).astype(jnp.int32))
    source = ((jnp.arange(N_GROUP, dtype=jnp.int32) - hop) % N_GROUP).astype(jnp.int32)
    new_params = 0.5 * (stepped + jnp.take(stepped, source, axis=0))
    return input_grad, new_params, new_momentum
```

```python
from functools import partial

import jax
import jax.numpy as jnp
from jax import lax
from jax.experimental import pallas as pl
from jax.experimental.pallas import tpu as pltpu
from jax.sharding import PartitionSpec as P

BF16 = jnp.bfloat16
F32 = jnp.float32
RING = 8
PAIR = 2
Z_GROUPS = [[PAIR * z + y for z in range(RING)] for y in range(PAIR)]
FIRST = (4, 3, -3)
SECOND = (2, -2, 1, -1, 0)


def along_z(part, by):
    length = RING * PAIR
    return lax.ppermute(part, "fsdp", [(i, (i + PAIR * by) % length) for i in range(length)])


def across_pair(part):
    return lax.ppermute(part, "fsdp", [(i, i ^ 1) for i in range(RING * PAIR)])


def along_group(part, by):
    length = lax.axis_size("group")
    return lax.ppermute(part, "group", [(i, (i + by) % length) for i in range(length)])


def split_kernel(where_ref, features_ref, mine_ref, theirs_ref):
    half = mine_ref.shape[2]
    low = features_ref[:, :half]
    high = features_ref[:, half:]
    even = where_ref[0] == 0
    mine_ref[0] = jnp.where(even, low, high)
    theirs_ref[0] = jnp.where(even, high, low)


def split_features(features, place, distances):
    tokens, width = features.shape
    block = width // RING
    half = block // PAIR
    count = len(distances)
    where = jnp.concatenate(
        [place[1:], (place[0] + jnp.array(distances, jnp.int32)) % RING]
    )
    out = jax.ShapeDtypeStruct((count, tokens, half), features.dtype)
    return pl.pallas_call(
        split_kernel,
        grid_spec=pltpu.PrefetchScalarGridSpec(
            num_scalar_prefetch=1,
            grid=(count,),
            in_specs=[pl.BlockSpec((tokens, block), lambda i, where_ref: (0, where_ref[1 + i]))],
            out_specs=[pl.BlockSpec((1, tokens, half), lambda i, where_ref: (i, 0, 0))] * 2,
        ),
        out_shape=[out, out],
        cost_estimate=pl.CostEstimate(
            flops=0, bytes_accessed=4 * count * tokens * block, transcendentals=0
        ),
    )(where, features)


def product_kernel(cotan_ref, weights_ref, out_ref):
    out_ref[0] = lax.dot_general(
        cotan_ref[...],
        weights_ref[0],
        (((1,), (1,)), ((), ())),
        preferred_element_type=F32,
    ).astype(out_ref.dtype)


def product(cotan, weights):
    tokens, depth = cotan.shape
    count, rows, _ = weights.shape
    return pl.pallas_call(
        product_kernel,
        grid=(count,),
        in_specs=[
            pl.BlockSpec((tokens, depth), lambda i: (0, 0)),
            pl.BlockSpec((1, rows, depth), lambda i: (i, 0, 0)),
        ],
        out_specs=pl.BlockSpec((1, tokens, rows), lambda i: (i, 0, 0)),
        out_shape=jax.ShapeDtypeStruct((count, tokens, rows), BF16),
        cost_estimate=pl.CostEstimate(
            flops=2 * count * tokens * depth * rows,
            bytes_accessed=2 * (tokens * depth + count * rows * (depth + tokens)),
            transcendentals=0,
        ),
    )(cotan, weights)


def join_kernel(where_ref, cotan_ref, weights_ref, arrived_ref, out_ref):
    own = lax.dot_general(
        cotan_ref[...],
        weights_ref[0],
        (((1,), (1,)), ((), ())),
        preferred_element_type=F32,
    ).astype(out_ref.dtype)
    other = arrived_ref[0]
    half = own.shape[1]
    even = where_ref[1] == 0
    out_ref[:, :half] = jnp.where(even, own, other)
    out_ref[:, half:] = jnp.where(even, other, own)


def product_and_join(cotan, weights, arrived, place):
    tokens, depth = cotan.shape
    count, rows, _ = weights.shape
    return pl.pallas_call(
        join_kernel,
        grid_spec=pltpu.PrefetchScalarGridSpec(
            num_scalar_prefetch=1,
            grid=(count,),
            in_specs=[
                pl.BlockSpec((tokens, depth), lambda i, _: (0, 0)),
                pl.BlockSpec((1, rows, depth), lambda i, _: (i, 0, 0)),
                pl.BlockSpec((1, tokens, rows), lambda i, _: (i, 0, 0)),
            ],
            out_specs=pl.BlockSpec((tokens, PAIR * rows), lambda i, _: (0, i)),
        ),
        out_shape=jax.ShapeDtypeStruct((tokens, count * PAIR * rows), BF16),
        cost_estimate=pl.CostEstimate(
            flops=2 * count * tokens * depth * rows,
            bytes_accessed=2 * (tokens * depth + count * rows * (depth + 3 * tokens)),
            transcendentals=0,
        ),
    )(place, cotan, weights, arrived)


def ring_sum(term, up, down):
    total = term(0)
    for far, sign in ((up, 1), (down, -1)):
        carried = term(sign * far)
        for distance in range(far - 1, -1, -1):
            arrived = along_z(carried.astype(BF16), sign).astype(F32)
            if distance:
                carried = term(sign * distance) + arrived
            else:
                total = total + arrived
    return total


def step(features, cotan, weights, moment, hop):
    index = lax.axis_index("fsdp")
    place = jnp.stack([index // PAIR, index % PAIR]).astype(jnp.int32)
    tokens, width = cotan.shape
    rows = weights.shape[0]

    gathered = lax.all_gather(
        weights.astype(BF16), "fsdp", axis_index_groups=Z_GROUPS, axis=0, tiled=True
    ).reshape(RING, rows, width)

    cotan_pair = jnp.concatenate([cotan, across_pair(cotan)], axis=0)
    blocks = {}
    for distances in (FIRST, SECOND):
        mine, theirs = split_features(features, place, distances)
        arrived = across_pair(theirs)
        for i, distance in enumerate(distances):
            blocks[distance % RING] = jnp.concatenate([mine[i], arrived[i]], axis=0)

    half = width // 2
    new_params, new_momentum = [], []
    for part, (up, down) in enumerate(((4, 3), (3, 4))):
        cut = slice(part * half, (part + 1) * half)

        def term(distance, cut=cut):
            return lax.dot_general(
                blocks[distance % RING],
                cotan_pair[:, cut],
                (((0,), (0,)), ((), ())),
                preferred_element_type=F32,
            )

        gradient = ring_sum(term, up, down) / (tokens * RING * PAIR)
        momentum = 0.9 * moment[:, cut] + gradient
        stepped = weights[:, cut] - 0.5 * momentum
        arrived = along_group(stepped.astype(BF16), hop).astype(F32)
        new_momentum.append(momentum)
        new_params.append(0.5 * (stepped + arrived))

    for_partner = product(cotan_pair[tokens:], gathered)
    input_grad = product_and_join(cotan, gathered, across_pair(for_partner), place)
    return (
        input_grad,
        jnp.concatenate(new_params, axis=1),
        jnp.concatenate(new_momentum, axis=1),
    )


def per_device(features, value_cotangent, params, momentum, step_index):
    levels = lax.axis_size("group").bit_length() - 1
    branches = [partial(step, hop=2**level) for level in range(levels)]
    outs = lax.switch(
        step_index[0] % levels,
        branches,
        features[0],
        value_cotangent[0],
        params[0],
        momentum[0],
    )
    return tuple(out[None] for out in outs)


def solution(mesh):
    in_specs = (
        P("group", "fsdp", None),
        P("group", "fsdp", None),
        P("group", "fsdp", None),
        P("group", "fsdp", None),
        P(),
    )
    out_specs = (P("group", "fsdp", None), P("group", "fsdp", None), P("group", "fsdp", None))
    return jax.shard_map(
        per_device, mesh=mesh, in_specs=in_specs, out_specs=out_specs, check_vma=False
    )
```

```python
from functools import partial

import jax
import jax.numpy as jnp
from jax import lax
from jax.experimental import pallas as pl
from jax.experimental.pallas import tpu as pltpu
from jax.sharding import PartitionSpec as P

BF16 = jnp.bfloat16
F32 = jnp.float32
RING = 8
PAIR = 2
FAR = RING // 2
KERNEL_BYTES = 8 * 1024 * 1024
ANY = pl.BlockSpec(memory_space=pl.ANY)
VMEM = pl.BlockSpec(memory_space=pltpu.VMEM)
TOKEN = jax.ShapeDtypeStruct((8, 128), F32)
PARAMS = pltpu.CompilerParams(vmem_limit_bytes=KERNEL_BYTES)

ROUNDS = tuple(
    zip(
        ("wb1", "wa1", "wb2", "wa2", "wb3", "wa3", "wb4", "sa1", "sb1", "sa2", "sb2", "sa3", "sb3", "sa4"),
        ("wa1", "wb1", "wa2", "wb2", "wa3", "wb3", "wa4", "sb1", "sa1", "sb2", "sa2", "sb3", "sa3", "sb4"),
        strict=True,
    )
)
G1, G2 = 6, 9
PRODUCTS = ((1, 4), (2, 5), (3, 7), (FAR, 8))
JOINS = (9, 10, 11, 12)
EARLY = None
REACH = {"wa": (3, 4), "wb": (4, 3), "sa": (4, 3), "sb": (3, 4)}
SIGNS = (1, -1)
SIDES = "ab"
FIRST = (FAR, FAR - 1, 1 - FAR)
SECOND = (2, -2, 1, -1, 0)


def along_z(part, by):
    length = RING * PAIR
    return lax.ppermute(part, "fsdp", [(i, (i + PAIR * by) % length) for i in range(length)])


def across_pair(part):
    return lax.ppermute(part, "fsdp", [(i, i ^ 1) for i in range(RING * PAIR)])


def along_group(part, by):
    length = lax.axis_size("group")
    return lax.ppermute(part, "group", [(i, (i + by) % length) for i in range(length)])


def cost(flops, touched):
    return pl.CostEstimate(flops=flops, bytes_accessed=touched, transcendentals=0)


def here():
    index = lax.axis_index("fsdp")
    ahead = (index // PAIR + jnp.arange(RING, dtype=jnp.int32)) % RING
    return jnp.concatenate([(index % PAIR)[None], ahead]).astype(jnp.int32)


def block_at(where_ref, i, distances):
    at = distances[-1] % RING
    for j, distance in enumerate(distances[:-1]):
        at = jnp.where(i == j, distance % RING, at)
    return where_ref[1 + at]


def in_vmem(kernel, operands, after, outs, flops=0, aliases=None):
    inputs = len(operands)

    def body(*refs):
        kernel(*refs[:inputs], *refs[inputs + len(after) : -1])
        refs[-1][...] = jnp.zeros(TOKEN.shape, TOKEN.dtype)

    return pl.pallas_call(
        body,
        in_specs=[VMEM] * (inputs + len(after)),
        out_specs=[VMEM] * (len(outs) + 1),
        out_shape=[*(jax.ShapeDtypeStruct(shape, kind) for shape, kind in outs), TOKEN],
        input_output_aliases=aliases or {},
        compiler_params=PARAMS,
        cost_estimate=cost(flops, 0),
    )(*operands, *after)


def serve(passed, sums, after):
    count = len(passed)

    def kernel(*refs):
        ins, outs = refs[: count + 2 * len(sums)], refs[count + 2 * len(sums) :]
        for k in range(count):
            outs[k][...] = ins[k][...]
        for k in range(len(sums)):
            term_ref, arrived_ref = ins[count + 2 * k : count + 2 * k + 2]
            outs[count + k][...] = (term_ref[...] + arrived_ref[...].astype(F32)).astype(BF16)

    operands = [*passed, *(part for pair in sums for part in pair)]
    outs = [(a.shape, a.dtype) for a in passed] + [(a.shape, BF16) for _, a in sums]
    *made, token = in_vmem(kernel, operands, after, outs, 0, {k: k for k in range(count)})
    return made[:count], made[count:], token


def split_kernel(where_ref, features_ref, *refs):
    mine_ref, theirs_ref, token_ref = refs[-3:]
    half = mine_ref.shape[0]
    turned = features_ref[...].T
    even = where_ref[0] == 0
    mine_ref[...] = jnp.where(even, turned[:half], turned[half:])
    theirs_ref[...] = jnp.where(even, turned[half:], turned[:half])
    token_ref[...] = jnp.zeros(TOKEN.shape, TOKEN.dtype)


def split_features(features, where, distances, after):
    tokens, width = features.shape
    block = width // RING
    half = block // PAIR
    count = len(distances)
    out = jax.ShapeDtypeStruct((count * half, tokens), features.dtype)
    return pl.pallas_call(
        split_kernel,
        grid_spec=pltpu.PrefetchScalarGridSpec(
            num_scalar_prefetch=1,
            grid=(count,),
            in_specs=[
                pl.BlockSpec(
                    (tokens, block), lambda i, where_ref: (0, block_at(where_ref, i, distances))
                ),
                *[VMEM] * len(after),
            ],
            out_specs=[pl.BlockSpec((half, tokens), lambda i, where_ref: (i, 0))] * 2 + [VMEM],
        ),
        out_shape=[out, out, TOKEN],
        compiler_params=PARAMS,
        cost_estimate=cost(0, 4 * count * tokens * block),
    )(where, features, *after)


def terms(mine, theirs, cotans, kinds, after):
    own, other = cotans
    tokens, width = own.shape
    count = len(kinds)
    rows = mine.shape[0] // count
    half = width // 2

    def kernel(mine_ref, theirs_ref, own_ref, other_ref, *out_refs):
        for i in range(count):
            block = slice(i * rows, (i + 1) * rows)
            for j in range(2):
                cut = slice(j * half, (j + 1) * half)
                out_ref = out_refs[2 * i + j]
                out_ref[...] = (
                    jnp.dot(mine_ref[block, :], own_ref[:, cut], preferred_element_type=F32)
                    + jnp.dot(theirs_ref[block, :], other_ref[:, cut], preferred_element_type=F32)
                ).astype(out_ref.dtype)

    outs = [((rows, half), kind) for pair in kinds for kind in pair]
    *made, token = in_vmem(
        kernel, [mine, theirs, own, other], after, outs, 4 * count * tokens * rows * width
    )
    return [tuple(made[2 * i : 2 * i + 2]) for i in range(count)], token


def products(cotans, weights, after):
    own, other = cotans
    tokens, depth = own.shape
    half = depth // 2
    count = len(weights)
    rows = weights[0][0].shape[0]

    def kernel(own_ref, other_ref, *refs):
        for i in range(count):
            for cotan_ref, out_ref in ((other_ref, refs[-1]), (own_ref, refs[-2])):
                total = sum(
                    lax.dot_general(
                        cotan_ref[:, j * half : (j + 1) * half],
                        refs[2 * i + j][...],
                        (((1,), (1,)), ((), ())),
                        preferred_element_type=F32,
                    )
                    for j in range(2)
                )
                out_ref[:, i * rows : (i + 1) * rows] = total.astype(BF16)

    return in_vmem(
        kernel,
        [own, other, *(part for block in weights for part in block)],
        after,
        [((tokens, count * rows), BF16)] * 2,
        4 * count * tokens * depth * rows,
    )


def join(own, arrived, where, distances, into, after):
    tokens, width = own.shape
    count = len(distances)
    rows = width // count

    def kernel(where_ref, own_ref, arrived_ref, *refs):
        out_ref, token_ref = refs[-2:]
        even = where_ref[0] == 0
        token_ref[...] = jnp.zeros(TOKEN.shape, TOKEN.dtype)
        for i in range(count):

            @pl.when(pl.program_id(0) == i)
            def _(i=i):
                cut = slice(i * rows, (i + 1) * rows)
                mine, theirs = own_ref[:, cut], arrived_ref[:, cut]
                out_ref[:, :rows] = jnp.where(even, mine, theirs)
                out_ref[:, rows:] = jnp.where(even, theirs, mine)

    whole = pl.BlockSpec((tokens, width), lambda i, where_ref: (0, 0))
    operands, in_specs, aliases = [own, arrived, *after], [whole, whole, *[VMEM] * len(after)], {}
    if into is not None:
        operands.append(into)
        in_specs.append(ANY)
        aliases = {len(operands): 0}
    return pl.pallas_call(
        kernel,
        grid_spec=pltpu.PrefetchScalarGridSpec(
            num_scalar_prefetch=1,
            grid=(count,),
            in_specs=in_specs,
            out_specs=[
                pl.BlockSpec(
                    (tokens, PAIR * rows),
                    lambda i, where_ref: (0, block_at(where_ref, i, distances)),
                ),
                VMEM,
            ],
        ),
        out_shape=[jax.ShapeDtypeStruct((tokens, RING * PAIR * rows), BF16), TOKEN],
        input_output_aliases=aliases,
        compiler_params=PARAMS,
        cost_estimate=cost(0, 8 * count * tokens * rows),
    )(where, *operands)


def settle(own, arrived, moment, side, count, after):
    rows, half = own.shape
    cut = slice(side * half, (side + 1) * half)

    def kernel(own_ref, arrived_ref, moment_ref, out_ref):
        total = own_ref[...] + arrived_ref[...].astype(F32)
        out_ref[...] = 0.9 * moment_ref[:, cut] + total / count

    return in_vmem(kernel, [own, arrived, moment], after, [((rows, half), F32)])


def update(settled, arrived, weights, sides, before, count, after):
    rows, half = settled[0].shape
    cuts = [slice(side * half, (side + 1) * half) for side in sides]

    def kernel(*refs):
        settled_refs, arrived_refs = refs[: len(sides)], refs[len(sides) : 2 * len(sides)]
        weights_ref = refs[2 * len(sides)]
        momentum_ref, stepped_ref, short_ref = refs[-3:]
        if before is not None:
            momentum_ref[:, :half] = refs[2 * len(sides) + 1][...]
        for k, cut in enumerate(cuts):
            momentum = settled_refs[k][...] + arrived_refs[k][...].astype(F32) / count
            stepped = weights_ref[:, cut] - 0.5 * momentum
            to = slice(k * half, (k + 1) * half)
            momentum_ref[:, cut if before is not None else to] = momentum
            stepped_ref[:, to] = stepped
            short_ref[:, to] = stepped.astype(BF16)

    operands = [*settled, *arrived, weights]
    width = len(sides) * half
    full = weights.shape[1] if before is not None else width
    if before is not None:
        operands.append(before)
    outs = [((rows, full), F32), ((rows, width), F32), ((rows, width), BF16)]
    return in_vmem(kernel, operands, after, outs)


def mix(stepped, arrived, before=None):
    rows, width = stepped.shape
    first = 0 if before is None else before.shape[1]

    def kernel(stepped_ref, arrived_ref, *refs):
        if before is not None:
            refs[-1][:, :first] = refs[0][...]
        refs[-1][:, first:] = 0.5 * (stepped_ref[...] + arrived_ref[...].astype(F32))

    operands = [stepped, arrived] if before is None else [stepped, arrived, before]
    return in_vmem(kernel, operands, (), [((rows, first + width), F32)])


def gossip(short, level, hops):
    return lax.switch(level, [partial(along_group, by=by) for by in hops], short)


def step(features, cotan, weights, moment, level, hops):
    where = here()
    tokens, width = cotan.shape
    half = width // 2
    count = tokens * RING * PAIR
    own = {side: weights[:, j * half : (j + 1) * half].astype(BF16) for j, side in enumerate(SIDES)}
    cotans = (cotan, across_pair(cotan))

    term, held, landed, flying = {}, {0: (own["a"], own["b"])}, {}, {}
    more = new_params = input_grad = None
    pieces = []

    def payload(side_way, name):
        chain, number = name[:2], int(name[2])
        if number > 1:
            arrived = landed.get((side_way, chain + str(number - 1)))
            if chain[0] == "w":
                return arrived, None
            left = REACH[chain][side_way] - number + 1
            return arrived, term[SIGNS[side_way] * left][SIDES.index(chain[1])]
        if chain[0] == "w":
            return own[chain[1]], None
        far = REACH[chain][side_way]
        return term[far if far == FAR else SIGNS[side_way] * far][SIDES.index(chain[1])], None

    mine, theirs, token = split_features(features, where, FIRST, ())
    blocks = (mine, across_pair(theirs))
    after = [token]
    for number in range(len(ROUNDS)):
        if number >= 2:
            names = [(way, ROUNDS[number - 2][way]) for way in range(2)]
            arrays = [flying[name] for name in names]
            landed.update(zip(names, arrays, strict=True))
            sums, kept = [], {}
            for way in range(2):
                array, addend = payload(way, ROUNDS[number][way])
                if addend is None:
                    kept[way] = array
                else:
                    sums.append((addend, array))
            passed, keys = [], []
            for key, array in [*zip(names, arrays, strict=True), *kept.items()]:
                if not any(array is one for one in passed) and not any(array is pair[1] for pair in sums):
                    passed.append(array)
                    keys.append(key)
            extra = []
            if number == 3:
                extra = [cotans[1]]
            if number == G1:
                extra = [blocks[1]]
            if number == G2:
                extra = [more[1]]
            handed, summed, token = serve([*passed, *extra], sums, after)
            if number == 3:
                cotans = (cotan, handed[-1])
            if number == G1:
                blocks = (mine, handed[-1])
            if number == G2:
                more = (more[0], handed[-1])
            after = [token]
            again = {id(a): b for a, b in zip(passed, handed)}
            for name in names:
                landed[name] = again.get(id(landed[name]))
            sends = []
            for way in range(2):
                sends.append(again[id(kept[way])] if way in kept else summed.pop(0))
            for way in range(2):
                name = ROUNDS[number][way]
                if way in kept and name[0] == "w" and name[2] != "1":
                    landed[way, name[:2] + str(int(name[2]) - 1)] = sends[way]
        else:
            sends = [payload(way, ROUNDS[number][way])[0] for way in range(2)]
        for way in range(2):
            flying[way, ROUNDS[number][way]] = along_z(sends[way], SIGNS[way])

        for distance, at in PRODUCTS:
            if at != number:
                continue
            some = (0, FAR) if distance == FAR else (distance, -distance)
            for d in some[1:] if distance == FAR else some:
                up, down = (0, 1) if d == FAR else ((1, 1) if d > 0 else (0, 0))
                key = str(abs(d))
                if d == FAR:
                    held[d] = (landed[1, "wa" + key], landed[0, "wb" + key])
                else:
                    held[d] = (landed[up, "wa" + key], landed[up, "wb" + key])
            ours, others, token = products(cotans, [held[d] for d in some], after)
            after = [token]
            pieces.append((ours, across_pair(others), some))
        if number == 2:
            rest, theirs, token = split_features(features, where, SECOND, after)
            more = (rest, across_pair(theirs))
            after = [token]
        if number == G1:
            kinds = ((BF16, BF16), (F32, BF16), (BF16, F32))
            made, token = terms(*blocks, cotans, kinds, after)
            term.update(zip(FIRST, made, strict=True))
            after = [token]
        if number == G2:
            made, token = terms(*more, cotans, ((F32, F32),) * 5, after)
            term.update(zip(SECOND, made, strict=True))
            after = [token]
        if number in JOINS:
            ours, others, some = pieces.pop(0)
            input_grad, token = join(ours, others, where, some, input_grad, after)
            after = [token]
        if number == EARLY:
            left, token = settle(term[0][0], landed[1, "sa3"], moment, 0, count, after)
            before, stepped, short, token = update(
                [left], [landed[0, "sa4"]], weights, (0,), None, count, [token]
            )
            new_params, token = mix(stepped, gossip(short, level, hops))
            after = [token]

    if EARLY:
        right, token = settle(term[0][1], flying[0, "sb3"], moment, 1, count, after)
        momentum, stepped, short, _ = update(
            [right], [flying[1, "sb4"]], weights, (1,), before, count, [token]
        )
    else:
        (up, down), _, token = serve([flying[0, "sb3"], flying[1, "sa3"]], [], after)
        left, token = settle(term[0][0], down, moment, 0, count, [token])
        right, token = settle(term[0][1], up, moment, 1, count, [token])
        arrived = [flying[0, "sa4"], flying[1, "sb4"]]
        momentum, stepped, short, _ = update(
            [left, right], arrived, weights, (0, 1), None, count, [token]
        )
    new_params, _ = mix(stepped, gossip(short, level, hops), new_params)
    for ours, others, some in pieces:
        input_grad, _ = join(ours, others, where, some, input_grad, ())
    return input_grad, new_params, momentum


def per_device(features, value_cotangent, params, momentum, step_index):
    levels = lax.axis_size("group").bit_length() - 1
    outs = step(
        features[0],
        value_cotangent[0],
        params[0],
        momentum[0],
        step_index[0] % levels,
        [2**i for i in range(levels)],
    )
    return tuple(out[None] for out in outs)


def solution(mesh):
    in_specs = (
        P("group", "fsdp", None),
        P("group", "fsdp", None),
        P("group", "fsdp", None),
        P("group", "fsdp", None),
        P(),
    )
    out_specs = (P("group", "fsdp", None), P("group", "fsdp", None), P("group", "fsdp", None))
    return jax.shard_map(
        per_device, mesh=mesh, in_specs=in_specs, out_specs=out_specs, check_vma=False
    )
```

```python
from functools import partial

import jax
import jax.numpy as jnp
from jax import lax
from jax.experimental import pallas as pl
from jax.experimental.pallas import tpu as pltpu
from jax.sharding import PartitionSpec as P

BF16 = jnp.bfloat16
F32 = jnp.float32
RING = 8
PAIR = 2
FAR = RING // 2
KERNEL_BYTES = 8 * 1024 * 1024
ANY = pl.BlockSpec(memory_space=pl.ANY)
VMEM = pl.BlockSpec(memory_space=pltpu.VMEM)
TOKEN = jax.ShapeDtypeStruct((8, 128), F32)
PARAMS = pltpu.CompilerParams(vmem_limit_bytes=KERNEL_BYTES)

ROUNDS = tuple(
    zip(
        ("wb1", "wa1", "wb2", "wa2", "wb3", "wa3", "wb4", "sa1", "sb1", "sa2", "sb2", "sa3", "sb3", "sa4"),
        ("wa1", "wb1", "wa2", "wb2", "wa3", "wb3", "wa4", "sb1", "sa1", "sb2", "sa2", "sb3", "sa3", "sb4"),
        strict=True,
    )
)
G1, G2 = 6, 9
PRODUCTS = (((1, -1, 2, -2), 5), ((3, -3, 0, 4), 8))
JOINS = (11, 12)
SETTLE = 10
REACH = {"wa": (3, 4), "wb": (4, 3), "sa": (4, 3), "sb": (3, 4)}
SIGNS = (1, -1)
SIDES = "ab"
FIRST = (FAR, FAR - 1, 1 - FAR)
SECOND = (2, -2, 1, -1, 0)


def along_z(part, by):
    length = RING * PAIR
    return lax.ppermute(part, "fsdp", [(i, (i + PAIR * by) % length) for i in range(length)])


def across_pair(part):
    return lax.ppermute(part, "fsdp", [(i, i ^ 1) for i in range(RING * PAIR)])


def along_group(part, by):
    length = lax.axis_size("group")
    return lax.ppermute(part, "group", [(i, (i + by) % length) for i in range(length)])


def cost(flops, touched):
    return pl.CostEstimate(flops=flops, bytes_accessed=touched, transcendentals=0)


def here():
    index = lax.axis_index("fsdp")
    ahead = (index // PAIR + jnp.arange(RING, dtype=jnp.int32)) % RING
    return jnp.concatenate([(index % PAIR)[None], ahead]).astype(jnp.int32)


def block_at(where_ref, i, distances):
    at = distances[-1] % RING
    for j, distance in enumerate(distances[:-1]):
        at = jnp.where(i == j, distance % RING, at)
    return where_ref[1 + at]


def in_vmem(kernel, operands, after, outs, flops=0, aliases=None):
    inputs = len(operands)

    def body(*refs):
        kernel(*refs[:inputs], *refs[inputs + len(after) : -1])
        refs[-1][...] = jnp.zeros(TOKEN.shape, TOKEN.dtype)

    return pl.pallas_call(
        body,
        in_specs=[VMEM] * (inputs + len(after)),
        out_specs=[VMEM] * (len(outs) + 1),
        out_shape=[*(jax.ShapeDtypeStruct(shape, kind) for shape, kind in outs), TOKEN],
        input_output_aliases=aliases or {},
        compiler_params=PARAMS,
        cost_estimate=cost(flops, 0),
    )(*operands, *after)


def serve(passed, sums, after):
    count = len(passed)

    def kernel(*refs):
        ins, outs = refs[: count + 2 * len(sums)], refs[count + 2 * len(sums) :]
        for k in range(count):
            outs[k][...] = ins[k][...]
        for k in range(len(sums)):
            term_ref, arrived_ref = ins[count + 2 * k : count + 2 * k + 2]
            outs[count + k][...] = (term_ref[...] + arrived_ref[...].astype(F32)).astype(BF16)

    operands = [*passed, *(part for pair in sums for part in pair)]
    outs = [(a.shape, a.dtype) for a in passed] + [(a.shape, BF16) for _, a in sums]
    *made, token = in_vmem(kernel, operands, after, outs, 0, {k: k for k in range(count)})
    return made[:count], made[count:], token


def split_kernel(where_ref, features_ref, *refs):
    mine_ref, theirs_ref, token_ref = refs[-3:]
    half = mine_ref.shape[0]
    turned = features_ref[...].T
    even = where_ref[0] == 0
    mine_ref[...] = jnp.where(even, turned[:half], turned[half:])
    theirs_ref[...] = jnp.where(even, turned[half:], turned[:half])
    token_ref[...] = jnp.zeros(TOKEN.shape, TOKEN.dtype)


def split_features(features, where, distances, after):
    tokens, width = features.shape
    block = width // RING
    half = block // PAIR
    count = len(distances)
    out = jax.ShapeDtypeStruct((count * half, tokens), features.dtype)
    return pl.pallas_call(
        split_kernel,
        grid_spec=pltpu.PrefetchScalarGridSpec(
            num_scalar_prefetch=1,
            grid=(count,),
            in_specs=[
                pl.BlockSpec(
                    (tokens, block), lambda i, where_ref: (0, block_at(where_ref, i, distances))
                ),
                *[VMEM] * len(after),
            ],
            out_specs=[pl.BlockSpec((half, tokens), lambda i, where_ref: (i, 0))] * 2 + [VMEM],
        ),
        out_shape=[out, out, TOKEN],
        compiler_params=PARAMS,
        cost_estimate=cost(0, 4 * count * tokens * block),
    )(where, features, *after)


def terms(mine, theirs, cotans, kinds, after):
    own, other = cotans
    tokens, width = own.shape
    count = len(kinds)
    rows = mine.shape[0] // count
    half = width // 2

    def kernel(mine_ref, theirs_ref, own_ref, other_ref, *out_refs):
        for i in range(count):
            block = slice(i * rows, (i + 1) * rows)
            for j in range(2):
                cut = slice(j * half, (j + 1) * half)
                out_ref = out_refs[2 * i + j]
                out_ref[...] = (
                    jnp.dot(mine_ref[block, :], own_ref[:, cut], preferred_element_type=F32)
                    + jnp.dot(theirs_ref[block, :], other_ref[:, cut], preferred_element_type=F32)
                ).astype(out_ref.dtype)

    outs = [((rows, half), kind) for pair in kinds for kind in pair]
    *made, token = in_vmem(
        kernel, [mine, theirs, own, other], after, outs, 4 * count * tokens * rows * width
    )
    return [tuple(made[2 * i : 2 * i + 2]) for i in range(count)], token


def products(cotans, weights, after):
    own, other = cotans
    tokens, depth = own.shape
    half = depth // 2
    count = len(weights)
    rows = weights[0][0].shape[0]

    def kernel(own_ref, other_ref, *refs):
        for i in range(count):
            for cotan_ref, out_ref in ((other_ref, refs[-1]), (own_ref, refs[-2])):
                total = sum(
                    lax.dot_general(
                        cotan_ref[:, j * half : (j + 1) * half],
                        refs[2 * i + j][...],
                        (((1,), (1,)), ((), ())),
                        preferred_element_type=F32,
                    )
                    for j in range(2)
                )
                out_ref[:, i * rows : (i + 1) * rows] = total.astype(BF16)

    return in_vmem(
        kernel,
        [own, other, *(part for block in weights for part in block)],
        after,
        [((tokens, count * rows), BF16)] * 2,
        4 * count * tokens * depth * rows,
    )


def join(own, arrived, where, distances, into, after):
    tokens, width = own.shape
    count = len(distances)
    rows = width // count

    def kernel(where_ref, own_ref, arrived_ref, *refs):
        out_ref, token_ref = refs[-2:]
        even = where_ref[0] == 0
        token_ref[...] = jnp.zeros(TOKEN.shape, TOKEN.dtype)
        for i in range(count):

            @pl.when(pl.program_id(0) == i)
            def _(i=i):
                cut = slice(i * rows, (i + 1) * rows)
                mine, theirs = own_ref[:, cut], arrived_ref[:, cut]
                out_ref[:, :rows] = jnp.where(even, mine, theirs)
                out_ref[:, rows:] = jnp.where(even, theirs, mine)

    whole = pl.BlockSpec((tokens, width), lambda i, where_ref: (0, 0))
    operands, in_specs, aliases = [own, arrived, *after], [whole, whole, *[VMEM] * len(after)], {}
    if into is not None:
        operands.append(into)
        in_specs.append(ANY)
        aliases = {len(operands): 0}
    return pl.pallas_call(
        kernel,
        grid_spec=pltpu.PrefetchScalarGridSpec(
            num_scalar_prefetch=1,
            grid=(count,),
            in_specs=in_specs,
            out_specs=[
                pl.BlockSpec(
                    (tokens, PAIR * rows),
                    lambda i, where_ref: (0, block_at(where_ref, i, distances)),
                ),
                VMEM,
            ],
        ),
        out_shape=[jax.ShapeDtypeStruct((tokens, RING * PAIR * rows), BF16), TOKEN],
        input_output_aliases=aliases,
        compiler_params=PARAMS,
        cost_estimate=cost(0, 8 * count * tokens * rows),
    )(where, *operands)


def shorten(weights):
    rows, width = weights.shape
    half = width // 2

    def kernel(weights_ref, left_ref, right_ref):
        left_ref[...] = weights_ref[:, :half].astype(BF16)
        right_ref[...] = weights_ref[:, half:].astype(BF16)

    return in_vmem(kernel, [weights], (), [((rows, half), BF16)] * 2)[:2]


def settle(own, moment, count, after):
    rows, half = own[0].shape

    def kernel(left_ref, right_ref, moment_ref, out_ref):
        out_ref[:, :half] = 0.9 * moment_ref[:, :half] + left_ref[...] / count
        out_ref[:, half:] = 0.9 * moment_ref[:, half:] + right_ref[...] / count

    return in_vmem(kernel, [*own, moment], after, [(moment.shape, F32)])


def fold(settled, arrived, weights, count, after):
    rows, width = weights.shape
    half = width // 2

    def kernel(settled_ref, left_ref, right_ref, weights_ref, momentum_ref, stepped_ref):
        for j, arrived_ref in enumerate((left_ref, right_ref)):
            cut = slice(j * half, (j + 1) * half)
            momentum = settled_ref[:, cut] + arrived_ref[...].astype(F32) / count
            momentum_ref[:, cut] = momentum
            stepped_ref[:, cut] = weights_ref[:, cut] - 0.5 * momentum

    outs = [((rows, width), F32)] * 2
    return in_vmem(kernel, [settled, *arrived, weights], after, outs)


def stepped_short(stepped, arrived, count):
    rows, width = stepped.shape
    half = width // 2

    def kernel(stepped_ref, left_ref, right_ref, out_ref):
        for j, arrived_ref in enumerate((left_ref, right_ref)):
            cut = slice(j * half, (j + 1) * half)
            last = arrived_ref[...].astype(F32) / count
            out_ref[:, cut] = (stepped_ref[:, cut] - 0.5 * last).astype(BF16)

    return in_vmem(kernel, [stepped, *arrived], (), [((rows, width), BF16)])[0]


def mix(stepped, arrived):
    rows, width = stepped.shape
    tile = rows // 4

    def kernel(stepped_ref, arrived_ref, out_ref):
        out_ref[...] = 0.5 * (stepped_ref[...] + arrived_ref[...].astype(F32))

    block = pl.BlockSpec((tile, width), lambda i: (i, 0))
    return pl.pallas_call(
        kernel,
        grid=(4,),
        in_specs=[block, block],
        out_specs=block,
        out_shape=jax.ShapeDtypeStruct(stepped.shape, F32),
        compiler_params=PARAMS,
        cost_estimate=cost(0, 0),
    )(stepped, arrived)


def finish(short, settled, arrived, weights, by, count):
    other = along_group(short, by)
    momentum, stepped, _ = fold(settled, arrived, weights, count, ())
    return mix(stepped, other), momentum


def step(features, cotan, weights, moment, level, hops):
    where = here()
    tokens, width = cotan.shape
    count = tokens * RING * PAIR
    own = dict(zip(SIDES, shorten(weights), strict=True))
    cotans = (cotan, across_pair(cotan))

    term, held, landed, flying = {}, {0: (own["a"], own["b"])}, {}, {}
    more = new_params = input_grad = None
    pieces = []

    def payload(side_way, name):
        chain, number = name[:2], int(name[2])
        if number > 1:
            arrived = landed.get((side_way, chain + str(number - 1)))
            if chain[0] == "w":
                return arrived, None
            left = REACH[chain][side_way] - number + 1
            return arrived, term[SIGNS[side_way] * left][SIDES.index(chain[1])]
        if chain[0] == "w":
            return own[chain[1]], None
        far = REACH[chain][side_way]
        return term[far if far == FAR else SIGNS[side_way] * far][SIDES.index(chain[1])], None

    mine, theirs, token = split_features(features, where, FIRST, ())
    blocks = (mine, across_pair(theirs))
    after = [token]
    for number in range(len(ROUNDS)):
        if number >= 2:
            names = [(way, ROUNDS[number - 2][way]) for way in range(2)]
            arrays = [flying[name] for name in names]
            landed.update(zip(names, arrays, strict=True))
            sums, kept = [], {}
            for way in range(2):
                array, addend = payload(way, ROUNDS[number][way])
                if addend is None:
                    kept[way] = array
                else:
                    sums.append((addend, array))
            passed, keys = [], []
            for key, array in [*zip(names, arrays, strict=True), *kept.items()]:
                if not any(array is one for one in passed) and not any(array is pair[1] for pair in sums):
                    passed.append(array)
                    keys.append(key)
            extra = []
            if number == 3:
                extra = [cotans[1]]
            if number == G1:
                extra = [blocks[1]]
            if number == G2:
                extra = [more[1]]
            handed, summed, token = serve([*passed, *extra], sums, after)
            if number == 3:
                cotans = (cotan, handed[-1])
            if number == G1:
                blocks = (mine, handed[-1])
            if number == G2:
                more = (more[0], handed[-1])
            after = [token]
            again = {id(a): b for a, b in zip(passed, handed)}
            for name in names:
                landed[name] = again.get(id(landed[name]))
            sends = []
            for way in range(2):
                sends.append(again[id(kept[way])] if way in kept else summed.pop(0))
            for way in range(2):
                name = ROUNDS[number][way]
                if way in kept and name[0] == "w" and name[2] != "1":
                    landed[way, name[:2] + str(int(name[2]) - 1)] = sends[way]
        else:
            sends = [payload(way, ROUNDS[number][way])[0] for way in range(2)]
        for way in range(2):
            flying[way, ROUNDS[number][way]] = along_z(sends[way], SIGNS[way])

        for some, at in PRODUCTS:
            if at != number:
                continue
            for d in some:
                key = str(abs(d))
                if d == FAR:
                    held[d] = (landed[1, "wa" + key], landed[0, "wb" + key])
                elif d:
                    way = 1 if d > 0 else 0
                    held[d] = (landed[way, "wa" + key], landed[way, "wb" + key])
            ours, others, token = products(cotans, [held[d] for d in some], after)
            after = [token]
            pieces.append((ours, across_pair(others), some))
        if number == 2:
            rest, theirs, token = split_features(features, where, SECOND, after)
            more = (rest, across_pair(theirs))
            after = [token]
        if number == G1:
            kinds = ((BF16, BF16), (F32, BF16), (BF16, F32))
            made, token = terms(*blocks, cotans, kinds, after)
            term.update(zip(FIRST, made, strict=True))
            after = [token]
        if number == G2:
            made, token = terms(*more, cotans, ((F32, F32),) * 5, after)
            term.update(zip(SECOND, made, strict=True))
            after = [token]
        if number in JOINS:
            ours, others, some = pieces.pop(0)
            input_grad, token = join(ours, others, where, some, input_grad, after)
            after = [token]
        if number == SETTLE:
            settled, token = settle(term[0], moment, count, after)
            after = [token]

    early = [flying[1, "sa3"], flying[0, "sb3"]]
    settled, stepped, _ = fold(settled, early, weights, count, after)
    arrived = [flying[0, "sa4"], flying[1, "sb4"]]
    short = stepped_short(stepped, arrived, count)
    branches = [partial(finish, by=by, count=count) for by in hops]
    new_params, momentum = lax.switch(level, branches, short, settled, arrived, weights)
    return input_grad, new_params, momentum


def per_device(features, value_cotangent, params, momentum, step_index):
    levels = lax.axis_size("group").bit_length() - 1
    outs = step(
        features[0],
        value_cotangent[0],
        params[0],
        momentum[0],
        step_index[0] % levels,
        [2**i for i in range(levels)],
    )
    return tuple(out[None] for out in outs)


def solution(mesh):
    in_specs = (
        P("group", "fsdp", None),
        P("group", "fsdp", None),
        P("group", "fsdp", None),
        P("group", "fsdp", None),
        P(),
    )
    out_specs = (P("group", "fsdp", None), P("group", "fsdp", None), P("group", "fsdp", None))
    return jax.shard_map(
        per_device, mesh=mesh, in_specs=in_specs, out_specs=out_specs, check_vma=False
    )
```

```python
from functools import partial

import jax
import jax.numpy as jnp
from jax import lax
from jax.experimental import pallas as pl
from jax.experimental.pallas import tpu as pltpu
from jax.sharding import PartitionSpec as P

BF16 = jnp.bfloat16
F32 = jnp.float32
RING = 8
PAIR = 2
FAR = RING // 2
KERNEL_BYTES = 8 * 1024 * 1024
ANY = pl.BlockSpec(memory_space=pl.ANY)
VMEM = pl.BlockSpec(memory_space=pltpu.VMEM)
TOKEN = jax.ShapeDtypeStruct((8, 128), F32)
PARAMS = pltpu.CompilerParams(vmem_limit_bytes=KERNEL_BYTES)

ROUNDS = tuple(
    zip(
        ("wb1", "wa1", "wb2", "wa2", "wb3", "wa3", "wb4", "sa1", "sb1", "sa2", "sb2", "sa3", "sb3", "sa4"),
        ("wa1", "wb1", "wa2", "wb2", "wa3", "wb3", "wa4", "sb1", "sa1", "sb2", "sa2", "sb3", "sa3", "sb4"),
        strict=True,
    )
)
G1, G2 = 6, 9
PRODUCTS = (((1, -1, 2, -2), 5), ((3, -3, 0, 4), 8))
JOINS = (11, 12)
SETTLE = 10
REACH = {"wa": (3, 4), "wb": (4, 3), "sa": (4, 3), "sb": (3, 4)}
SIGNS = (1, -1)
SIDES = "ab"
FIRST = (FAR, FAR - 1, 1 - FAR)
SECOND = (2, -2, 1, -1, 0)


def along_z(part, by):
    length = RING * PAIR
    return lax.ppermute(part, "fsdp", [(i, (i + PAIR * by) % length) for i in range(length)])


def across_pair(part):
    return lax.ppermute(part, "fsdp", [(i, i ^ 1) for i in range(RING * PAIR)])


def along_group(part, by):
    length = lax.axis_size("group")
    return lax.ppermute(part, "group", [(i, (i + by) % length) for i in range(length)])


def cost(flops, touched):
    return pl.CostEstimate(flops=flops, bytes_accessed=touched, transcendentals=0)


def here():
    index = lax.axis_index("fsdp")
    ahead = (index // PAIR + jnp.arange(RING, dtype=jnp.int32)) % RING
    return jnp.concatenate([(index % PAIR)[None], ahead]).astype(jnp.int32)


def block_at(where_ref, i, distances):
    at = distances[-1] % RING
    for j, distance in enumerate(distances[:-1]):
        at = jnp.where(i == j, distance % RING, at)
    return where_ref[1 + at]


def in_vmem(kernel, operands, after, outs, flops=0, aliases=None):
    inputs = len(operands)

    def body(*refs):
        kernel(*refs[:inputs], *refs[inputs + len(after) : -1])
        refs[-1][...] = jnp.zeros(TOKEN.shape, TOKEN.dtype)

    return pl.pallas_call(
        body,
        in_specs=[VMEM] * (inputs + len(after)),
        out_specs=[VMEM] * (len(outs) + 1),
        out_shape=[*(jax.ShapeDtypeStruct(shape, kind) for shape, kind in outs), TOKEN],
        input_output_aliases=aliases or {},
        compiler_params=PARAMS,
        cost_estimate=cost(flops, 0),
    )(*operands, *after)


def by_tiles(rows, body, tile=32):
    @pl.loop(0, rows // tile)
    def _(i):
        body(pl.ds(pl.multiple_of(i * tile, tile), tile))


def serve(passed, sums, after):
    count = len(passed)

    def kernel(*refs):
        ins, outs = refs[: count + 2 * len(sums)], refs[count + 2 * len(sums) :]
        for k in range(count):

            def copy(tile, k=k):
                outs[k][tile, :] = ins[k][tile, :]

            by_tiles(passed[k].shape[0], copy)
        for k, (_, arrived) in enumerate(sums):
            term_ref, arrived_ref = ins[count + 2 * k : count + 2 * k + 2]

            def add(tile, k=k, term_ref=term_ref, arrived_ref=arrived_ref):
                total = term_ref[tile, :] + arrived_ref[tile, :].astype(F32)
                outs[count + k][tile, :] = total.astype(BF16)

            by_tiles(arrived.shape[0], add)

    operands = [*passed, *(part for pair in sums for part in pair)]
    outs = [(a.shape, a.dtype) for a in passed] + [(a.shape, BF16) for _, a in sums]
    *made, token = in_vmem(kernel, operands, after, outs, 0, {k: k for k in range(count)})
    return made[:count], made[count:], token


def split_kernel(where_ref, features_ref, *refs):
    mine_ref, theirs_ref, token_ref = refs[-3:]
    half = mine_ref.shape[0]
    turned = features_ref[...].T
    even = where_ref[0] == 0
    mine_ref[...] = jnp.where(even, turned[:half], turned[half:])
    theirs_ref[...] = jnp.where(even, turned[half:], turned[:half])
    token_ref[...] = jnp.zeros(TOKEN.shape, TOKEN.dtype)


def split_features(features, where, distances, after):
    tokens, width = features.shape
    block = width // RING
    half = block // PAIR
    count = len(distances)
    out = jax.ShapeDtypeStruct((count * half, tokens), features.dtype)
    return pl.pallas_call(
        split_kernel,
        grid_spec=pltpu.PrefetchScalarGridSpec(
            num_scalar_prefetch=1,
            grid=(count,),
            in_specs=[
                pl.BlockSpec(
                    (tokens, block), lambda i, where_ref: (0, block_at(where_ref, i, distances))
                ),
                *[VMEM] * len(after),
            ],
            out_specs=[pl.BlockSpec((half, tokens), lambda i, where_ref: (i, 0))] * 2 + [VMEM],
        ),
        out_shape=[out, out, TOKEN],
        compiler_params=PARAMS,
        cost_estimate=cost(0, 4 * count * tokens * block),
    )(where, features, *after)


def terms(mine, theirs, cotans, kinds, after):
    own, other = cotans
    tokens, width = own.shape
    count = len(kinds)
    rows = mine.shape[0] // count
    half = width // 2

    def kernel(mine_ref, theirs_ref, own_ref, other_ref, *out_refs):
        for i in range(count):
            block = slice(i * rows, (i + 1) * rows)
            for j in range(2):
                cut = slice(j * half, (j + 1) * half)
                out_ref = out_refs[2 * i + j]
                out_ref[...] = (
                    jnp.dot(mine_ref[block, :], own_ref[:, cut], preferred_element_type=F32)
                    + jnp.dot(theirs_ref[block, :], other_ref[:, cut], preferred_element_type=F32)
                ).astype(out_ref.dtype)

    outs = [((rows, half), kind) for pair in kinds for kind in pair]
    *made, token = in_vmem(
        kernel, [mine, theirs, own, other], after, outs, 4 * count * tokens * rows * width
    )
    return [tuple(made[2 * i : 2 * i + 2]) for i in range(count)], token


def products(cotans, weights, after):
    own, other = cotans
    tokens, depth = own.shape
    half = depth // 2
    count = len(weights)
    rows = weights[0][0].shape[0]

    def kernel(own_ref, other_ref, *refs):
        for i in range(count):
            for cotan_ref, out_ref in ((other_ref, refs[-1]), (own_ref, refs[-2])):
                total = sum(
                    lax.dot_general(
                        cotan_ref[:, j * half : (j + 1) * half],
                        refs[2 * i + j][...],
                        (((1,), (1,)), ((), ())),
                        preferred_element_type=F32,
                    )
                    for j in range(2)
                )
                out_ref[:, i * rows : (i + 1) * rows] = total.astype(BF16)

    return in_vmem(
        kernel,
        [own, other, *(part for block in weights for part in block)],
        after,
        [((tokens, count * rows), BF16)] * 2,
        4 * count * tokens * depth * rows,
    )


def join(own, arrived, where, distances, into, after):
    tokens, width = own.shape
    count = len(distances)
    rows = width // count

    def kernel(where_ref, own_ref, arrived_ref, *refs):
        out_ref, token_ref = refs[-2:]
        even = where_ref[0] == 0
        token_ref[...] = jnp.zeros(TOKEN.shape, TOKEN.dtype)
        for i in range(count):

            @pl.when(pl.program_id(0) == i)
            def _(i=i):
                cut = slice(i * rows, (i + 1) * rows)
                mine, theirs = own_ref[:, cut], arrived_ref[:, cut]
                out_ref[:, :rows] = jnp.where(even, mine, theirs)
                out_ref[:, rows:] = jnp.where(even, theirs, mine)

    whole = pl.BlockSpec((tokens, width), lambda i, where_ref: (0, 0))
    operands, in_specs, aliases = [own, arrived, *after], [whole, whole, *[VMEM] * len(after)], {}
    if into is not None:
        operands.append(into)
        in_specs.append(ANY)
        aliases = {len(operands): 0}
    return pl.pallas_call(
        kernel,
        grid_spec=pltpu.PrefetchScalarGridSpec(
            num_scalar_prefetch=1,
            grid=(count,),
            in_specs=in_specs,
            out_specs=[
                pl.BlockSpec(
                    (tokens, PAIR * rows),
                    lambda i, where_ref: (0, block_at(where_ref, i, distances)),
                ),
                VMEM,
            ],
        ),
        out_shape=[jax.ShapeDtypeStruct((tokens, RING * PAIR * rows), BF16), TOKEN],
        input_output_aliases=aliases,
        compiler_params=PARAMS,
        cost_estimate=cost(0, 8 * count * tokens * rows),
    )(where, *operands)


def shorten(weights):
    rows, width = weights.shape
    half = width // 2

    def kernel(weights_ref, left_ref, right_ref):
        def short(tile):
            left_ref[tile, :] = weights_ref[tile, :half].astype(BF16)
            right_ref[tile, :] = weights_ref[tile, half:].astype(BF16)

        by_tiles(rows, short)

    return in_vmem(kernel, [weights], (), [((rows, half), BF16)] * 2)[:2]


def settle(own, moment, count, after):
    rows, half = own[0].shape

    def kernel(left_ref, right_ref, moment_ref, out_ref):
        def add(tile):
            out_ref[tile, :half] = 0.9 * moment_ref[tile, :half] + left_ref[tile, :] / count
            out_ref[tile, half:] = 0.9 * moment_ref[tile, half:] + right_ref[tile, :] / count

        by_tiles(rows, add)

    return in_vmem(kernel, [*own, moment], after, [(moment.shape, F32)])


def fold(settled, arrived, weights, count, after):
    rows, width = weights.shape
    half = width // 2

    def kernel(settled_ref, left_ref, right_ref, weights_ref, momentum_ref, stepped_ref):
        for j, arrived_ref in enumerate((left_ref, right_ref)):
            cut = slice(j * half, (j + 1) * half)

            def add(tile, cut=cut, arrived_ref=arrived_ref):
                momentum = settled_ref[tile, cut] + arrived_ref[tile, :].astype(F32) / count
                momentum_ref[tile, cut] = momentum
                stepped_ref[tile, cut] = weights_ref[tile, cut] - 0.5 * momentum

            by_tiles(rows, add)

    outs = [((rows, width), F32)] * 2
    return in_vmem(kernel, [settled, *arrived, weights], after, outs)


def stepped_short(stepped, arrived, count):
    rows, width = stepped.shape
    half = width // 2

    def kernel(stepped_ref, left_ref, right_ref, out_ref):
        for j, arrived_ref in enumerate((left_ref, right_ref)):
            cut = slice(j * half, (j + 1) * half)

            def add(tile, cut=cut, arrived_ref=arrived_ref):
                last = arrived_ref[tile, :].astype(F32) / count
                out_ref[tile, cut] = (stepped_ref[tile, cut] - 0.5 * last).astype(BF16)

            by_tiles(rows, add)

    return in_vmem(kernel, [stepped, *arrived], (), [((rows, width), BF16)])[0]


def mix(stepped, arrived):
    rows, width = stepped.shape
    tile = rows // 4

    def kernel(stepped_ref, arrived_ref, out_ref):
        def mean(rows):
            out_ref[rows, :] = 0.5 * (stepped_ref[rows, :] + arrived_ref[rows, :].astype(F32))

        by_tiles(tile, mean, 16)

    block = pl.BlockSpec((tile, width), lambda i: (i, 0))
    return pl.pallas_call(
        kernel,
        grid=(4,),
        in_specs=[block, block],
        out_specs=block,
        out_shape=jax.ShapeDtypeStruct(stepped.shape, F32),
        compiler_params=PARAMS,
        cost_estimate=cost(0, 0),
    )(stepped, arrived)


def finish(short, settled, arrived, weights, by, count):
    other = along_group(short, by)
    momentum, stepped, _ = fold(settled, arrived, weights, count, ())
    return mix(stepped, other), momentum


def step(features, cotan, weights, moment, level, hops):
    where = here()
    tokens, width = cotan.shape
    count = tokens * RING * PAIR
    own = dict(zip(SIDES, shorten(weights), strict=True))
    cotans = (cotan, across_pair(cotan))

    term, held, landed, flying = {}, {0: (own["a"], own["b"])}, {}, {}
    more = new_params = input_grad = None
    pieces = []

    def payload(side_way, name):
        chain, number = name[:2], int(name[2])
        if number > 1:
            arrived = landed.get((side_way, chain + str(number - 1)))
            if chain[0] == "w":
                return arrived, None
            left = REACH[chain][side_way] - number + 1
            return arrived, term[SIGNS[side_way] * left][SIDES.index(chain[1])]
        if chain[0] == "w":
            return own[chain[1]], None
        far = REACH[chain][side_way]
        return term[far if far == FAR else SIGNS[side_way] * far][SIDES.index(chain[1])], None

    mine, theirs, token = split_features(features, where, FIRST, ())
    blocks = (mine, across_pair(theirs))
    after = [token]
    for number in range(len(ROUNDS)):
        if number >= 2:
            names = [(way, ROUNDS[number - 2][way]) for way in range(2)]
            arrays = [flying[name] for name in names]
            landed.update(zip(names, arrays, strict=True))
            sums, kept = [], {}
            for way in range(2):
                array, addend = payload(way, ROUNDS[number][way])
                if addend is None:
                    kept[way] = array
                else:
                    sums.append((addend, array))
            passed, keys = [], []
            for key, array in [*zip(names, arrays, strict=True), *kept.items()]:
                if not any(array is one for one in passed) and not any(array is pair[1] for pair in sums):
                    passed.append(array)
                    keys.append(key)
            extra = []
            if number == 3:
                extra = [cotans[1]]
            if number == G1:
                extra = [blocks[1]]
            if number == G2:
                extra = [more[1]]
            handed, summed, token = serve([*passed, *extra], sums, after)
            if number == 3:
                cotans = (cotan, handed[-1])
            if number == G1:
                blocks = (mine, handed[-1])
            if number == G2:
                more = (more[0], handed[-1])
            after = [token]
            again = {id(a): b for a, b in zip(passed, handed)}
            for name in names:
                landed[name] = again.get(id(landed[name]))
            sends = []
            for way in range(2):
                sends.append(again[id(kept[way])] if way in kept else summed.pop(0))
            for way in range(2):
                name = ROUNDS[number][way]
                if way in kept and name[0] == "w" and name[2] != "1":
                    landed[way, name[:2] + str(int(name[2]) - 1)] = sends[way]
        else:
            sends = [payload(way, ROUNDS[number][way])[0] for way in range(2)]
        for way in range(2):
            flying[way, ROUNDS[number][way]] = along_z(sends[way], SIGNS[way])

        for some, at in PRODUCTS:
            if at != number:
                continue
            for d in some:
                key = str(abs(d))
                if d == FAR:
                    held[d] = (landed[1, "wa" + key], landed[0, "wb" + key])
                elif d:
                    way = 1 if d > 0 else 0
                    held[d] = (landed[way, "wa" + key], landed[way, "wb" + key])
            ours, others, token = products(cotans, [held[d] for d in some], after)
            after = [token]
            pieces.append((ours, across_pair(others), some))
        if number == 2:
            rest, theirs, token = split_features(features, where, SECOND, after)
            more = (rest, across_pair(theirs))
            after = [token]
        if number == G1:
            kinds = ((BF16, BF16), (F32, BF16), (BF16, F32))
            made, token = terms(*blocks, cotans, kinds, after)
            term.update(zip(FIRST, made, strict=True))
            after = [token]
        if number == G2:
            made, token = terms(*more, cotans, ((F32, F32),) * 5, after)
            term.update(zip(SECOND, made, strict=True))
            after = [token]
        if number in JOINS:
            ours, others, some = pieces.pop(0)
            input_grad, token = join(ours, others, where, some, input_grad, after)
            after = [token]
        if number == SETTLE:
            settled, token = settle(term[0], moment, count, after)
            after = [token]

    early = [flying[1, "sa3"], flying[0, "sb3"]]
    settled, stepped, _ = fold(settled, early, weights, count, after)
    arrived = [flying[0, "sa4"], flying[1, "sb4"]]
    short = stepped_short(stepped, arrived, count)
    branches = [partial(finish, by=by, count=count) for by in hops]
    new_params, momentum = lax.switch(level, branches, short, settled, arrived, weights)
    return input_grad, new_params, momentum


def per_device(features, value_cotangent, params, momentum, step_index):
    levels = lax.axis_size("group").bit_length() - 1
    outs = step(
        features[0],
        value_cotangent[0],
        params[0],
        momentum[0],
        step_index[0] % levels,
        [2**i for i in range(levels)],
    )
    return tuple(out[None] for out in outs)


def solution(mesh):
    in_specs = (
        P("group", "fsdp", None),
        P("group", "fsdp", None),
        P("group", "fsdp", None),
        P("group", "fsdp", None),
        P(),
    )
    out_specs = (P("group", "fsdp", None), P("group", "fsdp", None), P("group", "fsdp", None))
    return jax.shard_map(
        per_device, mesh=mesh, in_specs=in_specs, out_specs=out_specs, check_vma=False
    )
```

```python
from functools import partial

import jax
import jax.numpy as jnp
from jax import lax
from jax.experimental import pallas as pl
from jax.experimental.pallas import tpu as pltpu
from jax.sharding import PartitionSpec as P

BF16 = jnp.bfloat16
F32 = jnp.float32
RING = 8
PAIR = 2
FAR = RING // 2
KERNEL_BYTES = 8 * 1024 * 1024
ANY = pl.BlockSpec(memory_space=pl.ANY)
VMEM = pl.BlockSpec(memory_space=pltpu.VMEM)
TOKEN = jax.ShapeDtypeStruct((8, 128), F32)
PARAMS = pltpu.CompilerParams(vmem_limit_bytes=KERNEL_BYTES)

ROUNDS = tuple(
    zip(
        ("wb1", "wa1", "wb2", "wa2", "wb3", "wa3", "wb4", "sa1", "sb1", "sa2", "sb2", "sa3", "sb3", "sa4"),
        ("wa1", "wb1", "wa2", "wb2", "wa3", "wb3", "wa4", "sb1", "sa1", "sb2", "sa2", "sb3", "sa3", "sb4"),
        strict=True,
    )
)
G1, G2 = 6, 9
PRODUCTS = (((1, -1, 2, -2), 5), ((3, -3, 0, 4), 8))
JOINS = (11, 12)
SETTLE = 10
REACH = {"wa": (3, 4), "wb": (4, 3), "sa": (4, 3), "sb": (3, 4)}
SIGNS = (1, -1)
SIDES = "ab"
FIRST = (FAR, FAR - 1, 1 - FAR)
SECOND = (2, -2, 1, -1, 0)


def along_z(part, by):
    length = RING * PAIR
    return lax.ppermute(part, "fsdp", [(i, (i + PAIR * by) % length) for i in range(length)])


def across_pair(part):
    return lax.ppermute(part, "fsdp", [(i, i ^ 1) for i in range(RING * PAIR)])


def along_group(part, by):
    length = lax.axis_size("group")
    return lax.ppermute(part, "group", [(i, (i + by) % length) for i in range(length)])


def cost(flops, touched):
    return pl.CostEstimate(flops=flops, bytes_accessed=touched, transcendentals=0)


def here():
    index = lax.axis_index("fsdp")
    ahead = (index // PAIR + jnp.arange(RING, dtype=jnp.int32)) % RING
    return jnp.concatenate([(index % PAIR)[None], ahead]).astype(jnp.int32)


def block_at(where_ref, i, distances):
    at = distances[-1] % RING
    for j, distance in enumerate(distances[:-1]):
        at = jnp.where(i == j, distance % RING, at)
    return where_ref[1 + at]


def in_vmem(kernel, operands, after, outs, flops=0, aliases=None):
    inputs = len(operands)

    def body(*refs):
        kernel(*refs[:inputs], *refs[inputs + len(after) : -1])
        refs[-1][...] = jnp.zeros(TOKEN.shape, TOKEN.dtype)

    return pl.pallas_call(
        body,
        in_specs=[VMEM] * (inputs + len(after)),
        out_specs=[VMEM] * (len(outs) + 1),
        out_shape=[*(jax.ShapeDtypeStruct(shape, kind) for shape, kind in outs), TOKEN],
        input_output_aliases=aliases or {},
        compiler_params=PARAMS,
        cost_estimate=cost(flops, 0),
    )(*operands, *after)


def by_tiles(rows, body, tile=32):
    @pl.loop(0, rows // tile)
    def _(i):
        body(pl.ds(pl.multiple_of(i * tile, tile), tile))


def serve(passed, sums, after):
    count = len(passed)

    def kernel(*refs):
        ins, outs = refs[: count + 2 * len(sums)], refs[count + 2 * len(sums) :]
        for k in range(count):

            def copy(tile, k=k):
                outs[k][tile, :] = ins[k][tile, :]

            by_tiles(passed[k].shape[0], copy)
        for k, (_, arrived) in enumerate(sums):
            term_ref, arrived_ref = ins[count + 2 * k : count + 2 * k + 2]

            def add(tile, k=k, term_ref=term_ref, arrived_ref=arrived_ref):
                total = term_ref[tile, :] + arrived_ref[tile, :].astype(F32)
                outs[count + k][tile, :] = total.astype(BF16)

            by_tiles(arrived.shape[0], add)

    operands = [*passed, *(part for pair in sums for part in pair)]
    outs = [(a.shape, a.dtype) for a in passed] + [(a.shape, BF16) for _, a in sums]
    *made, token = in_vmem(kernel, operands, after, outs, 0, {k: k for k in range(count)})
    return made[:count], made[count:], token


def split_kernel(where_ref, features_ref, *refs):
    mine_ref, theirs_ref, token_ref = refs[-3:]
    half = mine_ref.shape[0]
    turned = features_ref[...].T
    even = where_ref[0] == 0
    mine_ref[...] = jnp.where(even, turned[:half], turned[half:])
    theirs_ref[...] = jnp.where(even, turned[half:], turned[:half])
    token_ref[...] = jnp.zeros(TOKEN.shape, TOKEN.dtype)


def split_features(features, where, distances, after):
    tokens, width = features.shape
    block = width // RING
    half = block // PAIR
    count = len(distances)
    out = jax.ShapeDtypeStruct((count * half, tokens), features.dtype)
    return pl.pallas_call(
        split_kernel,
        grid_spec=pltpu.PrefetchScalarGridSpec(
            num_scalar_prefetch=1,
            grid=(count,),
            in_specs=[
                pl.BlockSpec(
                    (tokens, block), lambda i, where_ref: (0, block_at(where_ref, i, distances))
                ),
                *[VMEM] * len(after),
            ],
            out_specs=[pl.BlockSpec((half, tokens), lambda i, where_ref: (i, 0))] * 2 + [VMEM],
        ),
        out_shape=[out, out, TOKEN],
        compiler_params=PARAMS,
        cost_estimate=cost(0, 4 * count * tokens * block),
    )(where, features, *after)


def terms(mine, theirs, cotans, kinds, after):
    own, other = cotans
    tokens, width = own.shape
    count = len(kinds)
    rows = mine.shape[0] // count
    half = width // 2

    def kernel(mine_ref, theirs_ref, own_ref, other_ref, *out_refs):
        for i in range(count):
            block = slice(i * rows, (i + 1) * rows)
            for j in range(2):
                cut = slice(j * half, (j + 1) * half)
                out_ref = out_refs[2 * i + j]
                out_ref[...] = (
                    jnp.dot(mine_ref[block, :], own_ref[:, cut], preferred_element_type=F32)
                    + jnp.dot(theirs_ref[block, :], other_ref[:, cut], preferred_element_type=F32)
                ).astype(out_ref.dtype)

    outs = [((rows, half), kind) for pair in kinds for kind in pair]
    *made, token = in_vmem(
        kernel, [mine, theirs, own, other], after, outs, 4 * count * tokens * rows * width
    )
    return [tuple(made[2 * i : 2 * i + 2]) for i in range(count)], token


def products(cotans, weights, after):
    own, other = cotans
    tokens, depth = own.shape
    half = depth // 2
    count = len(weights)
    rows = weights[0][0].shape[0]

    def kernel(own_ref, other_ref, *refs):
        for i in range(count):
            for cotan_ref, out_ref in ((other_ref, refs[-1]), (own_ref, refs[-2])):
                total = sum(
                    lax.dot_general(
                        cotan_ref[:, j * half : (j + 1) * half],
                        refs[2 * i + j][...],
                        (((1,), (1,)), ((), ())),
                        preferred_element_type=F32,
                    )
                    for j in range(2)
                )
                out_ref[:, i * rows : (i + 1) * rows] = total.astype(BF16)

    return in_vmem(
        kernel,
        [own, other, *(part for block in weights for part in block)],
        after,
        [((tokens, count * rows), BF16)] * 2,
        4 * count * tokens * depth * rows,
    )


def join(own, arrived, where, distances, into, after):
    tokens, width = own.shape
    count = len(distances)
    rows = width // count

    def kernel(where_ref, own_ref, arrived_ref, *refs):
        out_ref, token_ref = refs[-2:]
        even = where_ref[0] == 0
        token_ref[...] = jnp.zeros(TOKEN.shape, TOKEN.dtype)
        for i in range(count):

            @pl.when(pl.program_id(0) == i)
            def _(i=i):
                cut = slice(i * rows, (i + 1) * rows)
                mine, theirs = own_ref[:, cut], arrived_ref[:, cut]
                out_ref[:, :rows] = jnp.where(even, mine, theirs)
                out_ref[:, rows:] = jnp.where(even, theirs, mine)

    whole = pl.BlockSpec((tokens, width), lambda i, where_ref: (0, 0))
    operands, in_specs, aliases = [own, arrived, *after], [whole, whole, *[VMEM] * len(after)], {}
    if into is not None:
        operands.append(into)
        in_specs.append(ANY)
        aliases = {len(operands): 0}
    return pl.pallas_call(
        kernel,
        grid_spec=pltpu.PrefetchScalarGridSpec(
            num_scalar_prefetch=1,
            grid=(count,),
            in_specs=in_specs,
            out_specs=[
                pl.BlockSpec(
                    (tokens, PAIR * rows),
                    lambda i, where_ref: (0, block_at(where_ref, i, distances)),
                ),
                VMEM,
            ],
        ),
        out_shape=[jax.ShapeDtypeStruct((tokens, RING * PAIR * rows), BF16), TOKEN],
        input_output_aliases=aliases,
        compiler_params=PARAMS,
        cost_estimate=cost(0, 8 * count * tokens * rows),
    )(where, *operands)


def shorten(weights):
    rows, width = weights.shape
    half = width // 2

    def kernel(weights_ref, left_ref, right_ref):
        def short(tile):
            left_ref[tile, :] = weights_ref[tile, :half].astype(BF16)
            right_ref[tile, :] = weights_ref[tile, half:].astype(BF16)

        by_tiles(rows // 2, short)

    return pl.pallas_call(
        kernel,
        grid=(2,),
        in_specs=[pl.BlockSpec((rows // 2, width), lambda i: (i, 0))],
        out_specs=[pl.BlockSpec((rows // 2, half), lambda i: (i, 0))] * 2,
        out_shape=[jax.ShapeDtypeStruct((rows, half), BF16)] * 2,
        compiler_params=PARAMS,
        cost_estimate=cost(0, 0),
    )(weights)


def settle(own, moment, count, after):
    rows, half = own[0].shape

    def kernel(left_ref, right_ref, moment_ref, out_ref):
        def add(tile):
            out_ref[tile, :half] = 0.9 * moment_ref[tile, :half] + left_ref[tile, :] / count
            out_ref[tile, half:] = 0.9 * moment_ref[tile, half:] + right_ref[tile, :] / count

        by_tiles(rows, add)

    return in_vmem(kernel, [*own, moment], after, [(moment.shape, F32)])


def fold(settled, arrived, weights, count, after):
    rows, width = weights.shape
    half = width // 2

    def kernel(settled_ref, left_ref, right_ref, weights_ref, momentum_ref, stepped_ref):
        for j, arrived_ref in enumerate((left_ref, right_ref)):
            cut = slice(j * half, (j + 1) * half)

            def add(tile, cut=cut, arrived_ref=arrived_ref):
                momentum = settled_ref[tile, cut] + arrived_ref[tile, :].astype(F32) / count
                momentum_ref[tile, cut] = momentum
                stepped_ref[tile, cut] = weights_ref[tile, cut] - 0.5 * momentum

            by_tiles(rows, add)

    outs = [((rows, width), F32)] * 2
    return in_vmem(kernel, [settled, *arrived, weights], after, outs)


def stepped_short(stepped, arrived, count):
    rows, width = stepped.shape
    half = width // 2

    def kernel(stepped_ref, left_ref, right_ref, out_ref, *kept_refs):
        for j, arrived_ref in enumerate((left_ref, right_ref)):
            cut = slice(j * half, (j + 1) * half)

            def add(tile, cut=cut, arrived_ref=arrived_ref, kept_ref=kept_refs[j]):
                kept_ref[tile, :] = arrived_ref[tile, :]
                last = arrived_ref[tile, :].astype(F32) / count
                out_ref[tile, cut] = (stepped_ref[tile, cut] - 0.5 * last).astype(BF16)

            by_tiles(rows, add)

    outs = [((rows, width), BF16), *[((rows, half), BF16)] * 2]
    short, left, right, _ = in_vmem(kernel, [stepped, *arrived], (), outs)
    return short, (left, right)


def mix(stepped, arrived):
    rows, width = stepped.shape
    tile = rows // 4

    def kernel(stepped_ref, arrived_ref, out_ref):
        def mean(rows):
            out_ref[rows, :] = 0.5 * (stepped_ref[rows, :] + arrived_ref[rows, :].astype(F32))

        by_tiles(tile, mean, 16)

    block = pl.BlockSpec((tile, width), lambda i: (i, 0))
    return pl.pallas_call(
        kernel,
        grid=(4,),
        in_specs=[block, block],
        out_specs=block,
        out_shape=jax.ShapeDtypeStruct(stepped.shape, F32),
        compiler_params=PARAMS,
        cost_estimate=cost(0, 0),
    )(stepped, arrived)


def finish(short, settled, arrived, weights, by, count):
    other = along_group(short, by)
    momentum, stepped, _ = fold(settled, arrived, weights, count, ())
    return mix(stepped, other), momentum


def step(features, cotan, weights, moment, level, hops):
    where = here()
    tokens, width = cotan.shape
    count = tokens * RING * PAIR
    own = dict(zip(SIDES, shorten(weights), strict=True))
    cotans = (cotan, across_pair(cotan))

    term, held, landed, flying = {}, {0: (own["a"], own["b"])}, {}, {}
    more = new_params = input_grad = None
    pieces = []

    def payload(side_way, name):
        chain, number = name[:2], int(name[2])
        if number > 1:
            arrived = landed.get((side_way, chain + str(number - 1)))
            if chain[0] == "w":
                return arrived, None
            left = REACH[chain][side_way] - number + 1
            return arrived, term[SIGNS[side_way] * left][SIDES.index(chain[1])]
        if chain[0] == "w":
            return own[chain[1]], None
        far = REACH[chain][side_way]
        return term[far if far == FAR else SIGNS[side_way] * far][SIDES.index(chain[1])], None

    mine, theirs, token = split_features(features, where, FIRST, ())
    blocks = (mine, across_pair(theirs))
    after = [token]
    for number in range(len(ROUNDS)):
        if number >= 2:
            names = [(way, ROUNDS[number - 2][way]) for way in range(2)]
            arrays = [flying[name] for name in names]
            landed.update(zip(names, arrays, strict=True))
            sums, kept = [], {}
            for way in range(2):
                array, addend = payload(way, ROUNDS[number][way])
                if addend is None:
                    kept[way] = array
                else:
                    sums.append((addend, array))
            passed, keys = [], []
            for key, array in [*zip(names, arrays, strict=True), *kept.items()]:
                if not any(array is one for one in passed) and not any(array is pair[1] for pair in sums):
                    passed.append(array)
                    keys.append(key)
            extra = []
            if number == 3:
                extra = [cotans[1]]
            if number == G1:
                extra = [blocks[1]]
            if number == G2:
                extra = [more[1]]
            handed, summed, token = serve([*passed, *extra], sums, after)
            if number == 3:
                cotans = (cotan, handed[-1])
            if number == G1:
                blocks = (mine, handed[-1])
            if number == G2:
                more = (more[0], handed[-1])
            after = [token]
            again = {id(a): b for a, b in zip(passed, handed)}
            for name in names:
                landed[name] = again.get(id(landed[name]))
            sends = []
            for way in range(2):
                sends.append(again[id(kept[way])] if way in kept else summed.pop(0))
            for way in range(2):
                name = ROUNDS[number][way]
                if way in kept and name[0] == "w" and name[2] != "1":
                    landed[way, name[:2] + str(int(name[2]) - 1)] = sends[way]
        else:
            sends = [payload(way, ROUNDS[number][way])[0] for way in range(2)]
        for way in range(2):
            flying[way, ROUNDS[number][way]] = along_z(sends[way], SIGNS[way])

        for some, at in PRODUCTS:
            if at != number:
                continue
            for d in some:
                key = str(abs(d))
                if d == FAR:
                    held[d] = (landed[1, "wa" + key], landed[0, "wb" + key])
                elif d:
                    way = 1 if d > 0 else 0
                    held[d] = (landed[way, "wa" + key], landed[way, "wb" + key])
            ours, others, token = products(cotans, [held[d] for d in some], after)
            after = [token]
            pieces.append((ours, across_pair(others), some))
        if number == 2:
            rest, theirs, token = split_features(features, where, SECOND, after)
            more = (rest, across_pair(theirs))
            after = [token]
        if number == G1:
            kinds = ((BF16, BF16), (F32, BF16), (BF16, F32))
            made, token = terms(*blocks, cotans, kinds, after)
            term.update(zip(FIRST, made, strict=True))
            after = [token]
        if number == G2:
            made, token = terms(*more, cotans, ((F32, F32),) * 5, after)
            term.update(zip(SECOND, made, strict=True))
            after = [token]
        if number in JOINS:
            ours, others, some = pieces.pop(0)
            input_grad, token = join(ours, others, where, some, input_grad, after)
            after = [token]
        if number == SETTLE:
            settled, token = settle(term[0], moment, count, after)
            after = [token]

    early = [flying[1, "sa3"], flying[0, "sb3"]]
    settled, stepped, _ = fold(settled, early, weights, count, after)
    arrived = [flying[0, "sa4"], flying[1, "sb4"]]
    short, arrived = stepped_short(stepped, arrived, count)
    branches = [partial(finish, by=by, count=count) for by in hops]
    new_params, momentum = lax.switch(level, branches, short, settled, arrived, weights)
    return input_grad, new_params, momentum


def per_device(features, value_cotangent, params, momentum, step_index):
    levels = lax.axis_size("group").bit_length() - 1
    outs = step(
        features[0],
        value_cotangent[0],
        params[0],
        momentum[0],
        step_index[0] % levels,
        [2**i for i in range(levels)],
    )
    return tuple(out[None] for out in outs)


def solution(mesh):
    in_specs = (
        P("group", "fsdp", None),
        P("group", "fsdp", None),
        P("group", "fsdp", None),
        P("group", "fsdp", None),
        P(),
    )
    out_specs = (P("group", "fsdp", None), P("group", "fsdp", None), P("group", "fsdp", None))
    return jax.shard_map(
        per_device, mesh=mesh, in_specs=in_specs, out_specs=out_specs, check_vma=False
    )
```

```python
from functools import partial

import jax
import jax.numpy as jnp
from jax import lax
from jax.experimental import pallas as pl
from jax.experimental.pallas import tpu as pltpu
from jax.sharding import PartitionSpec as P

BF16 = jnp.bfloat16
F32 = jnp.float32
RING = 8
PAIR = 2
FAR = RING // 2
KERNEL_BYTES = 8 * 1024 * 1024
ANY = pl.BlockSpec(memory_space=pl.ANY)
VMEM = pl.BlockSpec(memory_space=pltpu.VMEM)
TOKEN = jax.ShapeDtypeStruct((8, 128), F32)
PARAMS = pltpu.CompilerParams(vmem_limit_bytes=KERNEL_BYTES)

ROUNDS = tuple(
    zip(
        ("wb1", "wa1", "wb2", "wa2", "wb3", "wa3", "wb4", "sa1", "sb1", "sa2", "sb2", "sa3", "sb3", "sa4"),
        ("wa1", "wb1", "wa2", "wb2", "wa3", "wb3", "wa4", "sb1", "sa1", "sb2", "sa2", "sb3", "sa3", "sb4"),
        strict=True,
    )
)
G1, G2 = 5, 8
PRODUCTS = (((1, -1, 2, -2), 5), ((3, -3, 0, 4), 9))
JOINS = (11, 13)
SETTLE = 12
REACH = {"wa": (3, 4), "wb": (4, 3), "sa": (4, 3), "sb": (3, 4)}
SIGNS = (1, -1)
SIDES = "ab"
FIRST = (FAR, FAR - 1, 1 - FAR)
SECOND = (2, -2, 1, -1, 0)


def along_z(part, by):
    length = RING * PAIR
    return lax.ppermute(part, "fsdp", [(i, (i + PAIR * by) % length) for i in range(length)])


def across_pair(part):
    return lax.ppermute(part, "fsdp", [(i, i ^ 1) for i in range(RING * PAIR)])


def along_group(part, by):
    length = lax.axis_size("group")
    return lax.ppermute(part, "group", [(i, (i + by) % length) for i in range(length)])


def cost(flops, touched):
    return pl.CostEstimate(flops=flops, bytes_accessed=touched, transcendentals=0)


def here():
    index = lax.axis_index("fsdp")
    ahead = (index // PAIR + jnp.arange(RING, dtype=jnp.int32)) % RING
    return jnp.concatenate([(index % PAIR)[None], ahead]).astype(jnp.int32)


def block_at(where_ref, i, distances):
    at = distances[-1] % RING
    for j, distance in enumerate(distances[:-1]):
        at = jnp.where(i == j, distance % RING, at)
    return where_ref[1 + at]


def in_vmem(kernel, operands, after, outs, flops=0, aliases=None):
    inputs = len(operands)

    def body(*refs):
        kernel(*refs[:inputs], *refs[inputs + len(after) : -1])
        refs[-1][...] = jnp.zeros(TOKEN.shape, TOKEN.dtype)

    return pl.pallas_call(
        body,
        in_specs=[VMEM] * (inputs + len(after)),
        out_specs=[VMEM] * (len(outs) + 1),
        out_shape=[*(jax.ShapeDtypeStruct(shape, kind) for shape, kind in outs), TOKEN],
        input_output_aliases=aliases or {},
        compiler_params=PARAMS,
        cost_estimate=cost(flops, 0),
    )(*operands, *after)


def by_tiles(rows, body, tile=32):
    @pl.loop(0, rows // tile)
    def _(i):
        body(pl.ds(pl.multiple_of(i * tile, tile), tile))


def serve(passed, sums, after):
    count = len(passed)

    def kernel(*refs):
        ins, outs = refs[: count + 2 * len(sums)], refs[count + 2 * len(sums) :]
        for k in range(count):

            def copy(tile, k=k):
                outs[k][tile, :] = ins[k][tile, :]

            by_tiles(passed[k].shape[0], copy)
        for k, (_, arrived) in enumerate(sums):
            term_ref, arrived_ref = ins[count + 2 * k : count + 2 * k + 2]

            def add(tile, k=k, term_ref=term_ref, arrived_ref=arrived_ref):
                total = term_ref[tile, :] + arrived_ref[tile, :].astype(F32)
                outs[count + k][tile, :] = total.astype(BF16)

            by_tiles(arrived.shape[0], add)

    operands = [*passed, *(part for pair in sums for part in pair)]
    outs = [(a.shape, a.dtype) for a in passed] + [(a.shape, BF16) for _, a in sums]
    *made, token = in_vmem(kernel, operands, after, outs, 0, {k: k for k in range(count)})
    return made[:count], made[count:], token


def split_kernel(where_ref, features_ref, *refs):
    mine_ref, theirs_ref, token_ref = refs[-3:]
    half = mine_ref.shape[0]
    turned = features_ref[...].T
    even = where_ref[0] == 0
    mine_ref[...] = jnp.where(even, turned[:half], turned[half:])
    theirs_ref[...] = jnp.where(even, turned[half:], turned[:half])
    token_ref[...] = jnp.zeros(TOKEN.shape, TOKEN.dtype)


def split_features(features, where, distances, after):
    tokens, width = features.shape
    block = width // RING
    half = block // PAIR
    count = len(distances)
    out = jax.ShapeDtypeStruct((count * half, tokens), features.dtype)
    return pl.pallas_call(
        split_kernel,
        grid_spec=pltpu.PrefetchScalarGridSpec(
            num_scalar_prefetch=1,
            grid=(count,),
            in_specs=[
                pl.BlockSpec(
                    (tokens, block), lambda i, where_ref: (0, block_at(where_ref, i, distances))
                ),
                *[VMEM] * len(after),
            ],
            out_specs=[pl.BlockSpec((half, tokens), lambda i, where_ref: (i, 0))] * 2 + [VMEM],
        ),
        out_shape=[out, out, TOKEN],
        compiler_params=PARAMS,
        cost_estimate=cost(0, 4 * count * tokens * block),
    )(where, features, *after)


def terms(mine, theirs, cotans, kinds, after):
    own, other = cotans
    tokens, width = own.shape
    count = len(kinds)
    rows = mine.shape[0] // count
    half = width // 2

    def kernel(mine_ref, theirs_ref, own_ref, other_ref, *out_refs):
        for i in range(count):
            block = slice(i * rows, (i + 1) * rows)
            for j in range(2):
                cut = slice(j * half, (j + 1) * half)
                out_ref = out_refs[2 * i + j]
                out_ref[...] = (
                    jnp.dot(mine_ref[block, :], own_ref[:, cut], preferred_element_type=F32)
                    + jnp.dot(theirs_ref[block, :], other_ref[:, cut], preferred_element_type=F32)
                ).astype(out_ref.dtype)

    outs = [((rows, half), kind) for pair in kinds for kind in pair]
    *made, token = in_vmem(
        kernel, [mine, theirs, own, other], after, outs, 4 * count * tokens * rows * width
    )
    return [tuple(made[2 * i : 2 * i + 2]) for i in range(count)], token


def products(cotans, weights, after):
    own, other = cotans
    tokens, depth = own.shape
    half = depth // 2
    count = len(weights)
    rows = weights[0][0].shape[0]

    def kernel(own_ref, other_ref, *refs):
        for i in range(count):
            for cotan_ref, out_ref in ((other_ref, refs[-1]), (own_ref, refs[-2])):
                total = sum(
                    lax.dot_general(
                        cotan_ref[:, j * half : (j + 1) * half],
                        refs[2 * i + j][...],
                        (((1,), (1,)), ((), ())),
                        preferred_element_type=F32,
                    )
                    for j in range(2)
                )
                out_ref[:, i * rows : (i + 1) * rows] = total.astype(BF16)

    return in_vmem(
        kernel,
        [own, other, *(part for block in weights for part in block)],
        after,
        [((tokens, count * rows), BF16)] * 2,
        4 * count * tokens * depth * rows,
    )


def join(own, arrived, where, distances, into, after):
    tokens, width = own.shape
    count = len(distances)
    rows = width // count

    def kernel(where_ref, own_ref, arrived_ref, *refs):
        out_ref, token_ref = refs[-2:]
        even = where_ref[0] == 0
        token_ref[...] = jnp.zeros(TOKEN.shape, TOKEN.dtype)
        for i in range(count):

            @pl.when(pl.program_id(0) == i)
            def _(i=i):
                cut = slice(i * rows, (i + 1) * rows)
                mine, theirs = own_ref[:, cut], arrived_ref[:, cut]
                out_ref[:, :rows] = jnp.where(even, mine, theirs)
                out_ref[:, rows:] = jnp.where(even, theirs, mine)

    whole = pl.BlockSpec((tokens, width), lambda i, where_ref: (0, 0))
    operands, in_specs, aliases = [own, arrived, *after], [whole, whole, *[VMEM] * len(after)], {}
    if into is not None:
        operands.append(into)
        in_specs.append(ANY)
        aliases = {len(operands): 0}
    return pl.pallas_call(
        kernel,
        grid_spec=pltpu.PrefetchScalarGridSpec(
            num_scalar_prefetch=1,
            grid=(count,),
            in_specs=in_specs,
            out_specs=[
                pl.BlockSpec(
                    (tokens, PAIR * rows),
                    lambda i, where_ref: (0, block_at(where_ref, i, distances)),
                ),
                VMEM,
            ],
        ),
        out_shape=[jax.ShapeDtypeStruct((tokens, RING * PAIR * rows), BF16), TOKEN],
        input_output_aliases=aliases,
        compiler_params=PARAMS,
        cost_estimate=cost(0, 8 * count * tokens * rows),
    )(where, *operands)


def shorten(weights):
    rows, width = weights.shape
    half = width // 2

    def kernel(weights_ref, left_ref, right_ref):
        def short(tile):
            left_ref[tile, :] = weights_ref[tile, :half].astype(BF16)
            right_ref[tile, :] = weights_ref[tile, half:].astype(BF16)

        by_tiles(rows // 2, short)

    return pl.pallas_call(
        kernel,
        grid=(2,),
        in_specs=[pl.BlockSpec((rows // 2, width), lambda i: (i, 0))],
        out_specs=[pl.BlockSpec((rows // 2, half), lambda i: (i, 0))] * 2,
        out_shape=[jax.ShapeDtypeStruct((rows, half), BF16)] * 2,
        compiler_params=PARAMS,
        cost_estimate=cost(0, 0),
    )(weights)


def settle(own, moment, count, after):
    rows, half = own[0].shape

    def kernel(left_ref, right_ref, moment_ref, out_ref):
        def add(tile):
            out_ref[tile, :half] = 0.9 * moment_ref[tile, :half] + left_ref[tile, :] / count
            out_ref[tile, half:] = 0.9 * moment_ref[tile, half:] + right_ref[tile, :] / count

        by_tiles(rows, add)

    return in_vmem(kernel, [*own, moment], after, [(moment.shape, F32)])


def fold(settled, arrived, weights, count, after):
    rows, width = weights.shape
    half = width // 2

    def kernel(settled_ref, left_ref, right_ref, weights_ref, momentum_ref, stepped_ref):
        for j, arrived_ref in enumerate((left_ref, right_ref)):
            cut = slice(j * half, (j + 1) * half)

            def add(tile, cut=cut, arrived_ref=arrived_ref):
                momentum = settled_ref[tile, cut] + arrived_ref[tile, :].astype(F32) / count
                momentum_ref[tile, cut] = momentum
                stepped_ref[tile, cut] = weights_ref[tile, cut] - 0.5 * momentum

            by_tiles(rows, add)

    outs = [((rows, width), F32)] * 2
    return in_vmem(kernel, [settled, *arrived, weights], after, outs)


def stepped_short(stepped, arrived, count):
    rows, width = stepped.shape
    half = width // 2

    def kernel(stepped_ref, left_ref, right_ref, out_ref, *kept_refs):
        for j, arrived_ref in enumerate((left_ref, right_ref)):
            cut = slice(j * half, (j + 1) * half)

            def add(tile, cut=cut, arrived_ref=arrived_ref, kept_ref=kept_refs[j]):
                kept_ref[tile, :] = arrived_ref[tile, :]
                last = arrived_ref[tile, :].astype(F32) / count
                out_ref[tile, cut] = (stepped_ref[tile, cut] - 0.5 * last).astype(BF16)

            by_tiles(rows, add)

    outs = [((rows, width), BF16), *[((rows, half), BF16)] * 2]
    short, left, right, _ = in_vmem(kernel, [stepped, *arrived], (), outs)
    return short, (left, right)


def mix(stepped, arrived):
    rows, width = stepped.shape
    tile = rows // 4

    def kernel(stepped_ref, arrived_ref, out_ref):
        def mean(rows):
            out_ref[rows, :] = 0.5 * (stepped_ref[rows, :] + arrived_ref[rows, :].astype(F32))

        by_tiles(tile, mean, 16)

    block = pl.BlockSpec((tile, width), lambda i: (i, 0))
    return pl.pallas_call(
        kernel,
        grid=(4,),
        in_specs=[block, block],
        out_specs=block,
        out_shape=jax.ShapeDtypeStruct(stepped.shape, F32),
        compiler_params=PARAMS,
        cost_estimate=cost(0, 0),
    )(stepped, arrived)


def finish(short, settled, arrived, weights, by, count):
    other = along_group(short, by)
    momentum, stepped, _ = fold(settled, arrived, weights, count, ())
    return mix(stepped, other), momentum


def step(features, cotan, weights, moment, level, hops):
    where = here()
    tokens, width = cotan.shape
    count = tokens * RING * PAIR
    own = dict(zip(SIDES, shorten(weights), strict=True))
    cotans = (cotan, across_pair(cotan))

    term, held, landed, flying = {}, {0: (own["a"], own["b"])}, {}, {}
    more = new_params = input_grad = None
    pieces = []

    def payload(side_way, name):
        chain, number = name[:2], int(name[2])
        if number > 1:
            arrived = landed.get((side_way, chain + str(number - 1)))
            if chain[0] == "w":
                return arrived, None
            left = REACH[chain][side_way] - number + 1
            return arrived, term[SIGNS[side_way] * left][SIDES.index(chain[1])]
        if chain[0] == "w":
            return own[chain[1]], None
        far = REACH[chain][side_way]
        return term[far if far == FAR else SIGNS[side_way] * far][SIDES.index(chain[1])], None

    mine, theirs, token = split_features(features, where, FIRST, ())
    blocks = (mine, across_pair(theirs))
    after = [token]
    for number in range(len(ROUNDS)):
        if number >= 2:
            names = [(way, ROUNDS[number - 2][way]) for way in range(2)]
            arrays = [flying[name] for name in names]
            landed.update(zip(names, arrays, strict=True))
            sums, kept = [], {}
            for way in range(2):
                array, addend = payload(way, ROUNDS[number][way])
                if addend is None:
                    kept[way] = array
                else:
                    sums.append((addend, array))
            passed, keys = [], []
            for key, array in [*zip(names, arrays, strict=True), *kept.items()]:
                if not any(array is one for one in passed) and not any(array is pair[1] for pair in sums):
                    passed.append(array)
                    keys.append(key)
            extra = []
            if number == 2:
                extra = [cotans[1]]
            if number == G1:
                extra = [blocks[1]]
            if number == G2:
                extra = [more[1], pieces[0][1]]
            if number == JOINS[0]:
                extra = [pieces[0][1], pieces[1][1]]
            handed, summed, token = serve([*passed, *extra], sums, after)
            after = [token]
            if number == 2:
                cotans = (cotan, handed[-1])
            if number == G1:
                blocks = (mine, handed[-1])
            if number == G2:
                more = (more[0], handed[-2])
                pieces[0][1] = across_pair(handed[-1])
            if number == JOINS[0]:
                pieces[0][1] = handed[-2]
                pieces[1][1] = across_pair(handed[-1])
            again = {id(a): b for a, b in zip(passed, handed)}
            for name in names:
                landed[name] = again.get(id(landed[name]))
            sends = []
            for way in range(2):
                sends.append(again[id(kept[way])] if way in kept else summed.pop(0))
            for way in range(2):
                name = ROUNDS[number][way]
                if way in kept and name[0] == "w" and name[2] != "1":
                    landed[way, name[:2] + str(int(name[2]) - 1)] = sends[way]
        else:
            sends = [payload(way, ROUNDS[number][way])[0] for way in range(2)]
        for way in range(2):
            flying[way, ROUNDS[number][way]] = along_z(sends[way], SIGNS[way])

        for some, at in PRODUCTS:
            if at != number:
                continue
            for d in some:
                key = str(abs(d))
                if d == FAR:
                    held[d] = (landed[1, "wa" + key], landed[0, "wb" + key])
                elif d:
                    way = 1 if d > 0 else 0
                    held[d] = (landed[way, "wa" + key], landed[way, "wb" + key])
            ours, others, token = products(cotans, [held[d] for d in some], after)
            after = [token]
            pieces.append([ours, others, some])
        if number == 2:
            rest, theirs, token = split_features(features, where, SECOND, after)
            more = (rest, across_pair(theirs))
            after = [token]
        if number == G1:
            kinds = ((BF16, BF16), (F32, BF16), (BF16, F32))
            made, token = terms(*blocks, cotans, kinds, after)
            term.update(zip(FIRST, made, strict=True))
            after = [token]
        if number == G2:
            made, token = terms(*more, cotans, ((F32, F32),) * 5, after)
            term.update(zip(SECOND, made, strict=True))
            after = [token]
        if number in JOINS:
            ours, others, some = pieces.pop(0)
            input_grad, token = join(ours, others, where, some, input_grad, after)
            after = [token]
        if number == SETTLE:
            settled, token = settle(term[0], moment, count, after)
            after = [token]

    early = [flying[1, "sa3"], flying[0, "sb3"]]
    settled, stepped, _ = fold(settled, early, weights, count, after)
    arrived = [flying[0, "sa4"], flying[1, "sb4"]]
    short, arrived = stepped_short(stepped, arrived, count)
    branches = [partial(finish, by=by, count=count) for by in hops]
    new_params, momentum = lax.switch(level, branches, short, settled, arrived, weights)
    return input_grad, new_params, momentum


def per_device(features, value_cotangent, params, momentum, step_index):
    levels = lax.axis_size("group").bit_length() - 1
    outs = step(
        features[0],
        value_cotangent[0],
        params[0],
        momentum[0],
        step_index[0] % levels,
        [2**i for i in range(levels)],
    )
    return tuple(out[None] for out in outs)


def solution(mesh):
    in_specs = (
        P("group", "fsdp", None),
        P("group", "fsdp", None),
        P("group", "fsdp", None),
        P("group", "fsdp", None),
        P(),
    )
    out_specs = (P("group", "fsdp", None), P("group", "fsdp", None), P("group", "fsdp", None))
    return jax.shard_map(
        per_device, mesh=mesh, in_specs=in_specs, out_specs=out_specs, check_vma=False
    )
```
